256 devices in a mesh: section: 16 (over z, core), tensor: 4 (over x), pool: 4 (over y).
Axes of the slice: x: 4, y: 4, z: 8, core: 2. Of those that a mesh axis runs over, the one named last changes fastest.
Arguments:
- acts: bfloat16 [16, 1536, 8192], P('section', None, 'tensor'), may hold values from -6 to 6
- output_weight: bfloat16 [16, 8192, 4096], P('section', 'tensor', 'pool'), may hold values from -0.0625 to 0.0625
- adapter_down_panels: bfloat16 [192, 64, 8192], P('section', 'pool', 'tensor'), may hold values from -0.0625 to 0.0625
- adapter_up_panels: bfloat16 [192, 64, 4096], P('section', 'tensor', 'pool'), may hold values from -0.75 to 0.75
- span_adapter_ids: int32 [16, 12], replicated, may hold values from 0 to 191, as said below
- segment_positions: int32 [16, 12], P('section'), may hold values from 0 to 11, each once within a row
- storage_slot_table: int32 [192], replicated, may hold values from 0 to 191, as said below
Outputs:
- handed: float32 [16, 1536, 4096], P('section', 'tensor', 'pool')
The draws below stay inside these ranges and needn't reach their ends.
Inputs may be any that keep to these rules, and one draw needn't show every extreme that they name: `storage_slot_table`: a permutation; storage slot i lies on section i // 12. `span_adapter_ids`: the ids of one section are distinct; for every section at most 2 of its ids have slots on one section, and exactly 2 on some section. `segment_positions`: each row is a permutation.
All inputs are finite; a program needn't handle non-finite values.
Results may differ from the reference program's by a relative error of at most 0.0003.
Values may be sent and summed in bfloat16 or wider, within the bound.
No kernel may reach another device: no remote copies, remote signals or barrier semaphores. Data moves between devices by JAX's collectives and lax.ppermute only.
A program may use at most 128 MiB of HBM per device.

```python
import jax
import jax.numpy as jnp
from jax import lax

MODEL_WIDTH = 8192
OUTPUT_FEATURES = 4096
ADAPTER_RANK = 64
SEG = 128
SPAN_ADP = 12
ADP_SECTION = 12
SECTIONS = 16
ADAPTER_COUNT = 192
SPAN_ROWS = 1536
CAP = 2


def request_tables(key):
    storage_slot_table = jax.random.permutation(jax.random.fold_in(key, 11), ADAPTER_COUNT).astype(jnp.int32)
    slot_owner = jnp.argsort(storage_slot_table, stable=True).astype(jnp.int32)
    seat_total = SECTIONS * CAP
    seat_section = jnp.arange(seat_total, dtype=jnp.int32) // CAP
    seat_rank = jnp.arange(seat_total, dtype=jnp.int32) % CAP

    def one_section(section_key):
        section_keys = jax.random.split(section_key, 4)
        hottest = jax.random.randint(section_keys[0], (), 0, SECTIONS).astype(jnp.int32)
        ranking = jax.random.permutation(section_keys[1], seat_total).astype(jnp.int32)
        priority = jnp.where(seat_section == hottest, -1, ranking)
        chosen = jnp.argsort(priority, stable=True)[:SPAN_ADP]
        local_keys = jax.random.split(section_keys[2], SECTIONS)
        local_table = jax.vmap(lambda one_key: jax.random.permutation(one_key, ADP_SECTION))(local_keys).astype(jnp.int32)
        owner_of = seat_section[chosen]
        inner_slot = local_table[owner_of, seat_rank[chosen]]
        slot_list = owner_of * ADP_SECTION + inner_slot
        chosen_ids = slot_owner[slot_list]
        return jax.random.permutation(section_keys[3], chosen_ids)
    span_adapter_ids = jax.vmap(one_section)(jax.random.split(jax.random.fold_in(key, 12), SECTIONS))
    return (storage_slot_table, span_adapter_ids.astype(jnp.int32))


def draw_storage_slot_table(key, part):
    tables = request_tables(key)
    return tables[0]


def draw_span_adapter_ids(key, part):
    tables = request_tables(key)
    return tables[1]


def shard_levels(stream_key, shape, cuts, low, largest):
    gain, own = 1.0, jax.random.fold_in(stream_key, 6)
    for dim, shards_of in cuts:
        heights = jnp.exp(jax.random.uniform(jax.random.fold_in(own, dim), (shards_of,), jnp.float32, low / len(cuts), largest / len(cuts)))
        gain = gain * jnp.repeat(heights, shape[dim] // shards_of).reshape([-1 if axis == dim else 1 for axis in range(len(shape))])
    return gain


def bell_draw(key, shape, deviation, limit, shards=(), kind=jnp.bfloat16):
    factor_of = shard_levels(key, shape, shards, -0.22, 0.18) if shards else 1.0
    values = jax.random.normal(key, shape, jnp.float32) * deviation * factor_of
    return jnp.minimum(jnp.maximum(values, -limit), limit).astype(kind)


def setup_inputs(seed: int = 0) -> dict:
    keys = jax.random.split(jax.random.key(seed), 8)
    acts = bell_draw(keys[0], (SECTIONS, SPAN_ROWS, MODEL_WIDTH), 1.0, 6.0, ((0, 16), (2, 4)))
    output_weight = bell_draw(keys[1], (SECTIONS, MODEL_WIDTH, OUTPUT_FEATURES), MODEL_WIDTH ** -0.5, 0.0625, ((0, 16), (1, 4), (2, 4)))
    adapter_down_panels = bell_draw(keys[2], (ADAPTER_COUNT, ADAPTER_RANK, MODEL_WIDTH), MODEL_WIDTH ** -0.5, 0.0625, ((0, 16), (1, 4), (2, 4)))
    adapter_up_panels = bell_draw(keys[3], (ADAPTER_COUNT, ADAPTER_RANK, OUTPUT_FEATURES), ADAPTER_RANK ** -0.5, 0.75, ((0, 16), (1, 4), (2, 4)))
    span_adapter_ids = draw_span_adapter_ids(jax.random.fold_in(keys[7], 71), 0)
    segment_positions = jax.vmap(lambda own: jax.random.permutation(own, SPAN_ADP))(jax.random.split(keys[5], SECTIONS)).reshape((SECTIONS, SPAN_ADP)).astype(jnp.int32)
    storage_slot_table = draw_storage_slot_table(jax.random.fold_in(keys[7], 71), 0)
    return {"acts": acts, "output_weight": output_weight, "adapter_down_panels": adapter_down_panels, "adapter_up_panels": adapter_up_panels, "span_adapter_ids": span_adapter_ids, "segment_positions": segment_positions, "storage_slot_table": storage_slot_table}


ADAPTER_SCALE = 2.0


def reference(acts, output_weight, adapter_down_panels, adapter_up_panels, span_adapter_ids, segment_positions, storage_slot_table):
    def one_section(section_idx):
        slot_ids = storage_slot_table[span_adapter_ids[section_idx]].astype(jnp.int32)
        segment_adapter = slot_ids[segment_positions[section_idx]].astype(jnp.int32)
        segment_down = adapter_down_panels[segment_adapter].astype(jnp.float32)
        expander_matrix = adapter_up_panels[segment_adapter].astype(jnp.float32)
        tokens = acts[section_idx]
        base_projection = jnp.dot(tokens, output_weight[section_idx], preferred_element_type=jnp.float32)
        blocks = tokens.astype(jnp.float32).reshape(SPAN_ADP, SEG, MODEL_WIDTH)
        bottleneck_signals = jnp.einsum("gsd,grd->gsr", blocks, segment_down, precision=lax.Precision.HIGHEST)
        correction_term = jnp.einsum("ryz,rzf->ryf", bottleneck_signals, expander_matrix, precision=lax.Precision.HIGHEST)
        return base_projection + ADAPTER_SCALE * correction_term.reshape(SPAN_ROWS, OUTPUT_FEATURES)

    combined_output = lax.map(one_section, jnp.arange(SECTIONS, dtype=jnp.int32))
    return jnp.roll(combined_output, 1, axis=0)
```

```python
import jax
import jax.numpy as jnp
from jax import lax
from jax.sharding import PartitionSpec as P

ADAPTER_SCALE = 2.0
LANES = 128
BLOCK = 16
STEPS = 128.0
TOP = 32767.0


def encode(x):
    rows, width = x.shape
    parts = x.reshape(rows // BLOCK, BLOCK, width)
    peak = jnp.maximum(jnp.max(jnp.abs(parts), axis=1), 2.0**-110)
    code = jnp.ceil(jnp.log2(peak) * STEPS) + 1.0
    inverse = jnp.exp2(code * (-1.0 / STEPS)) * TOP
    values = jnp.round(parts * inverse[:, None, :]).reshape(rows, width)
    pad = jnp.zeros(((-rows // BLOCK) % 16, width), jnp.float32)
    return jnp.concatenate([values, code, pad]).astype(jnp.int16)


def decode(sent, rows):
    width = sent.shape[1]
    count = rows // BLOCK
    code = sent[rows : rows + count].astype(jnp.float32)
    scale = jnp.exp2(code * (1.0 / STEPS)) * (1.0 / TOP)
    values = sent[:rows].astype(jnp.float32).reshape(count, BLOCK, width)
    return (values * scale[:, None, :]).reshape(rows, width)


def along(block, axis, distance):
    n = lax.axis_size(axis)
    return lax.ppermute(block, axis, [(i, (i + distance) % n) for i in range(n)])


def to_next_section(block, pool_distance):
    axes = ("section", "tensor", "pool")
    sections, tensors, pools = (lax.axis_size(a) for a in axes)
    route = [
        (
            (s * tensors + t) * pools + p,
            ((s + 1) % sections * tensors + t) * pools + (p + pool_distance) % pools,
        )
        for s in range(sections)
        for t in range(tensors)
        for p in range(pools)
    ]
    return lax.ppermute(block, axes, route)


def swap_all(block, axis):
    return lax.all_to_all(block, axis, split_axis=0, concat_axis=0, tiled=True)


def shards(acts, output_weight, down, up, ids, positions, table):
    sections, groups = lax.axis_size("section"), lax.axis_size("tensor")
    me_t, me_p = lax.axis_index("tensor"), lax.axis_index("pool")
    slots, ranks, width = down.shape
    columns = up.shape[2]
    spans = ids.shape[1]
    tokens, weight = acts[0], output_weight[0]
    rows = tokens.shape[0]
    share = rows // groups
    seg_rows = rows // spans
    own_segs = spans // groups
    half = ranks // 2

    piece_down = down.reshape(slots, ranks, sections, LANES).transpose(2, 0, 1, 3)
    piece_up = up.reshape(slots, 2, half, columns // LANES, LANES).transpose(3, 1, 0, 2, 4)
    pos_row = jnp.zeros((8, LANES), jnp.bfloat16).at[0, :spans].set(positions[0].astype(jnp.bfloat16))
    spread = jnp.concatenate(
        [
            piece_down.reshape(sections, slots * ranks, LANES),
            piece_up.reshape(sections, slots * half, LANES),
            jnp.broadcast_to(pos_row[None], (sections, 8, LANES)),
        ],
        axis=1,
    )
    held = swap_all(spread, "section")
    n_down, n_up = slots * ranks, slots * half
    held_down = held[:, :n_down].reshape(sections * slots, ranks, LANES)
    held_up = held[:, n_down : n_down + n_up].reshape(sections * slots, half, LANES)
    all_pos = held[:, n_down + n_up, :spans].astype(jnp.int32)

    adapters = table.shape[0]
    hit = ids[:, :, None] == jnp.arange(adapters, dtype=jnp.int32)
    slot_ids = jnp.sum(jnp.where(hit, table, 0), axis=-1)
    got_down = swap_all(
        held_down[slot_ids.reshape(-1)].reshape(sections, spans * ranks, LANES), "section"
    )
    seg_hit = all_pos[:, :, None] == jnp.arange(spans, dtype=jnp.int32)
    seg_slots = jnp.sum(jnp.where(seg_hit, slot_ids[:, None, :], 0), axis=-1)
    seg_slots = jnp.roll(seg_slots, 1, axis=0)
    got_up = swap_all(
        held_up[seg_slots.reshape(-1)].reshape(sections * groups, own_segs * half, LANES),
        ("section", "tensor"),
    )
    expander = (
        got_up.reshape(columns // LANES, 2, groups, own_segs, half, LANES)
        .transpose(3, 2, 1, 4, 0, 5)
        .reshape(own_segs, groups * ranks, columns)
    )

    full = jnp.dot(tokens, weight, preferred_element_type=jnp.float32)
    def rows_of(distance, part):
        start = (me_t + distance) % groups * share + part * (share // 2)
        return lax.dynamic_slice_in_dim(full, start, share // 2, 0)
    hs = share // 2
    far_up = along(encode(rows_of(2, 0)), "tensor", 1)
    far_down = along(encode(rows_of(2, 1)), "tensor", -1)
    near_up = along(encode(rows_of(1, 1)), "tensor", 1)
    near_down = along(encode(rows_of(-1, 0)), "tensor", -1)
    sum_up = along(encode(rows_of(1, 0) + decode(far_up, hs)), "tensor", 1)
    sum_down = along(encode(rows_of(-1, 1) + decode(far_down, hs)), "tensor", -1)
    first = rows_of(0, 0) + decode(near_down, hs) + decode(sum_up, hs)
    second = rows_of(0, 1) + decode(near_up, hs) + decode(sum_down, hs)
    base = to_next_section(encode(jnp.concatenate([first, second])), 0)

    panels = got_down.reshape(sections, spans * ranks, LANES).transpose(1, 0, 2).reshape(-1, width)
    products = lax.dot_general(
        panels, tokens, (((1,), (1,)), ((), ())), preferred_element_type=jnp.float32
    )
    mine = jnp.arange(spans, dtype=jnp.int32)[:, None] == positions[0][None, :]
    low = jnp.sum(
        jnp.where(
            mine[:, None, :, None], products.reshape(spans, ranks, spans, seg_rows), 0.0
        ),
        axis=0,
    ).reshape(ranks, rows)

    def low_of(distance):
        return lax.dynamic_slice_in_dim(low, (me_t + distance) % groups * share, share, 1)

    reduced = low_of(0)
    for distance in range(1, groups):
        reduced = reduced + along(low_of(distance), "tensor", distance)
    pools = lax.axis_size("pool")
    arrived = jnp.stack([to_next_section(reduced, k) for k in range(pools)])
    order = (me_p - jnp.arange(pools)) % pools
    low_full = arrived[order].reshape(pools * ranks, own_segs, seg_rows)

    upper = lax.optimization_barrier(low_full.astype(jnp.bfloat16))
    lower = (low_full - upper.astype(jnp.float32)).astype(jnp.bfloat16)
    correction = sum(
        jnp.einsum("rgi,grf->gif", part, expander, preferred_element_type=jnp.float32)
        for part in (upper, lower)
    )
    out = decode(base, share) + ADAPTER_SCALE * correction.reshape(share, columns)
    return out[None]


def solution(mesh):
    return jax.shard_map(
        shards,
        mesh=mesh,
        in_specs=(
            P("section", None, "tensor"),
            P("section", "tensor", "pool"),
            P("section", "pool", "tensor"),
            P("section", "tensor", "pool"),
            P(),
            P("section", None),
            P(),
        ),
        out_specs=P("section", "tensor", "pool"),
        check_vma=False,
    )
```

```python
import functools

import jax
import jax.numpy as jnp
from jax import lax
from jax.experimental import pallas as pl
from jax.experimental.pallas import tpu as pltpu
from jax.sharding import PartitionSpec as P

ADAPTER_SCALE = 2.0
LANES = 128
BLOCK = 16
STEPS = 128.0
TOP = 32767.0
LARGE = 56 * 2**20
COLUMNS = 256
CHEAP = pl.CostEstimate(flops=1000, bytes_accessed=1000, transcendentals=0)
LONG = pl.CostEstimate(flops=50_000_000_000, bytes_accessed=100_000_000, transcendentals=0)
bf16, f32, i16, i32 = jnp.bfloat16, jnp.float32, jnp.int16, jnp.int32


def coded_rows(rows):
    codes = rows // BLOCK
    return rows + (codes + 15) // 16 * 16


def nearest(x):
    return (x + 1.5 * 2.0**23) - 1.5 * 2.0**23


def encode(ref, cols, x):
    rows, width = x.shape
    tail = coded_rows(rows) - rows
    row = lax.broadcasted_iota(i32, (tail, width), 0)
    peaks = jnp.zeros((tail, width), f32)
    for b in range(rows // BLOCK):
        peak = jnp.max(jnp.abs(x[b * BLOCK : (b + 1) * BLOCK]), axis=0, keepdims=True)
        peaks = jnp.where(row == b, peak, peaks)
    codes = jnp.ceil(jnp.log2(jnp.maximum(peaks, 2.0**-110)) * STEPS) + 1.0
    inverse = jnp.exp2(codes * (-1.0 / STEPS)) * TOP
    for b in range(rows // BLOCK):
        part = x[b * BLOCK : (b + 1) * BLOCK] * inverse[b : b + 1]
        ref[b * BLOCK : (b + 1) * BLOCK, cols] = nearest(part).astype(i32).astype(i16)
    ref[rows:, cols] = codes.astype(i32).astype(i16)


def decode(ref, cols, rows):
    codes = ref[rows:, cols].astype(i32).astype(f32)
    scale = jnp.exp2(codes * (1.0 / STEPS)) * (1.0 / TOP)
    parts = []
    for b in range(rows // BLOCK):
        values = ref[b * BLOCK : (b + 1) * BLOCK, cols].astype(i32).astype(f32)
        parts.append(values * scale[b : b + 1])
    return jnp.concatenate(parts)


def along(block, axis, distance):
    n = lax.axis_size(axis)
    return lax.ppermute(block, axis, [(i, (i + distance) % n) for i in range(n)])


def to_next_section(block, pool_distance):
    axes = ("section", "tensor", "pool")
    sections, tensors, pools = (lax.axis_size(a) for a in axes)
    route = [
        (
            (s * tensors + t) * pools + p,
            ((s + 1) % sections * tensors + t) * pools + (p + pool_distance) % pools,
        )
        for s in range(sections)
        for t in range(tensors)
        for p in range(pools)
    ]
    return lax.ppermute(block, axes, route)


def swap_all(block, axis):
    return lax.all_to_all(block, axis, split_axis=0, concat_axis=0, tiled=True)


SCALARS = pl.BlockSpec(memory_space=pltpu.SMEM)
ARRAY = pl.BlockSpec(memory_space=pltpu.VMEM)
ANYWHERE = pl.BlockSpec(memory_space=pl.ANY)
HBM = pl.BlockSpec(memory_space=pltpu.HBM)


def call(
    kernel,
    out_shape,
    scalars,
    arrays,
    wait_for=(),
    in_specs=None,
    out_specs=None,
    scratch_shapes=(),
    vmem=8 * 2**20,
):
    first, waits = 1 + len(arrays), len(wait_for)

    def body(*refs):
        kernel(*refs[:first], *refs[first + waits :])

    many = isinstance(out_shape, list)
    return pl.pallas_call(
        body,
        out_shape=out_shape,
        in_specs=[SCALARS] + (in_specs or [ARRAY] * len(arrays)) + [ANYWHERE] * waits,
        out_specs=out_specs or ([ARRAY] * len(out_shape) if many else ARRAY),
        scratch_shapes=list(scratch_shapes),
        cost_estimate=CHEAP,
        compiler_params=pltpu.CompilerParams(vmem_limit_bytes=vmem),
    )(scalars, *arrays, *wait_for)


def for_columns(columns, body):
    def step(n, carry):
        body(pl.ds(pl.multiple_of(n * COLUMNS, COLUMNS), COLUMNS))
        return carry

    lax.fori_loop(0, columns // COLUMNS, step, 0)


def spread_pieces(down, up, positions):
    slots, ranks, width = down.shape
    columns = up.shape[2]
    half = ranks // 2
    n_down, n_up = slots * ranks, slots * half
    tiles = columns // LANES
    spans = positions.shape[0]

    def kernel(pos_ref, down_hbm, up_hbm, out_hbm, down_ref, up_ref, out_ref, sems):
        get_up = pltpu.make_async_copy(up_hbm, up_ref, sems.at[0])
        get_down = pltpu.make_async_copy(down_hbm, down_ref, sems.at[1])
        get_up.start()
        get_down.start()
        lane = lax.broadcasted_iota(i32, (16, LANES), 1)
        marks = jnp.zeros((16, LANES), i32)
        for j in range(spans):
            marks = jnp.where(lane == j, pos_ref[j], marks)
        marks = marks.astype(f32).astype(bf16)
        get_up.wait()
        for c in range(tiles):
            raised = up_ref[:, :, c * LANES : (c + 1) * LANES].astype(f32)
            for h in range(2):
                piece = raised[:, h * half : (h + 1) * half, :].reshape(n_up, LANES)
                out_ref[2 * c + h, n_down : n_down + n_up, :] = piece.astype(bf16)
                out_ref[2 * c + h, n_down + n_up :, :] = marks
        get_down.wait()
        puts = []
        for part in range(2):
            here = pl.ds(part * tiles, tiles)
            for i in range(part * tiles, (part + 1) * tiles):
                out_ref[i, :n_down, :] = down_ref[:, i * LANES : (i + 1) * LANES]
            puts.append(pltpu.make_async_copy(out_ref.at[here], out_hbm.at[here], sems.at[2 + part]))
            puts[part].start()
        for put in puts:
            put.wait()

    shape = (2 * tiles, n_down + n_up + 16, LANES)
    return call(
        kernel,
        jax.ShapeDtypeStruct(shape, bf16),
        positions,
        [down.reshape(n_down, width), up],
        vmem=LARGE,
        in_specs=[HBM] * 2,
        out_specs=HBM,
        scratch_shapes=[
            pltpu.VMEM((n_down, width), bf16),
            pltpu.VMEM(up.shape, bf16),
            pltpu.VMEM(shape, bf16),
            pltpu.SemaphoreType.DMA((4,)),
        ],
    )


def pick_down(held, tiles, ranks, wait_for):
    sections, total, _ = held.shape
    spans = tiles.shape[1]

    def kernel(tiles_ref, held_ref, out_ref):
        for r in range(sections):
            row = [held_ref[tiles_ref[r * spans + j]] for j in range(spans)]
            for j in range(spans):
                out_ref[r, j] = row[j]

    out = jax.ShapeDtypeStruct((sections, spans, ranks, LANES), bf16)
    split = held.reshape(sections * total // ranks, ranks, LANES)
    picked = call(kernel, out, tiles.reshape(-1), [split], wait_for)
    return picked.reshape(sections, spans * ranks, LANES)


def pick_up(held, seg_slots, slots, ranks, wait_for):
    sections, total, _ = held.shape
    spans = seg_slots.shape[1]
    half = ranks // 2
    first, count = slots * ranks, slots * half

    def kernel(ids_ref, held_ref, out_ref, wide):
        for o in range(sections):
            piece = held_ref[o, first : first + count, :].astype(f32)
            wide[o * slots : (o + 1) * slots] = piece.reshape(slots, half, LANES)
        for r in range(sections):
            row = [wide[ids_ref[r * spans + g]] for g in range(spans)]
            out_ref[r] = jnp.concatenate(row).astype(bf16)

    out = jax.ShapeDtypeStruct((sections, spans * half, LANES), bf16)
    wide = pltpu.VMEM((sections * slots, half, LANES), f32)
    return call(kernel, out, seg_slots.reshape(-1), [held], wait_for, scratch_shapes=[wide])


def dot(a, b):
    return jnp.dot(a, b, preferred_element_type=f32)


def by_columns(kernel, outs, me, arrays, wait_for, groups, columns, cost=CHEAP):
    waits = len(wait_for)

    def body(me_ref, *refs):
        kernel(me_ref, *refs[waits:])

    def rows_spec(tokens, distance):
        share = tokens.shape[0] // groups
        return pl.BlockSpec(
            (share, tokens.shape[1]), lambda n, me: ((me[0] + distance) % groups, 0)
        )

    def column_spec(array):
        return pl.BlockSpec((array.shape[0], COLUMNS), lambda n, me: (0, n))

    specs = [rows_spec(*x) if isinstance(x, tuple) else column_spec(x) for x in arrays]
    arrays = [x[0] if isinstance(x, tuple) else x for x in arrays]
    return pl.pallas_call(
        body,
        grid_spec=pltpu.PrefetchScalarGridSpec(
            num_scalar_prefetch=1,
            grid=(columns // COLUMNS,),
            in_specs=[ANYWHERE] * waits + specs,
            out_specs=[column_spec(x) for x in outs],
        ),
        out_shape=outs,
        cost_estimate=cost,
        compiler_params=pltpu.CompilerParams(vmem_limit_bytes=LARGE),
    )(me, *wait_for, *arrays)


EVERY = slice(None)


def far_sums(me, tokens, weight, groups, wait_for):
    part, columns = tokens.shape[0] // groups // 2, weight.shape[1]

    def kernel(me_ref, a_ref, w_ref, up_ref, down_ref):
        full = dot(a_ref[...], w_ref[...])
        encode(up_ref, EVERY, full[:part])
        encode(down_ref, EVERY, full[part:])

    coded = jax.ShapeDtypeStruct((coded_rows(part), columns), i16)
    arrays = [(tokens, 2), weight]
    return by_columns(kernel, [coded] * 2, me, arrays, wait_for, groups, columns)


def near_sums(me, tokens, weight, groups, wait_for):
    part, columns = tokens.shape[0] // groups // 2, weight.shape[1]

    def kernel(me_ref, a_up_ref, a_down_ref, w_ref, up_ref, down_ref, keep_up_ref, keep_down_ref):
        full = dot(a_up_ref[...], w_ref[...])
        keep_up_ref[...] = full[:part]
        encode(up_ref, EVERY, full[part:])
        full = dot(a_down_ref[...], w_ref[...])
        keep_down_ref[...] = full[part:]
        encode(down_ref, EVERY, full[:part])

    coded = jax.ShapeDtypeStruct((coded_rows(part), columns), i16)
    kept = jax.ShapeDtypeStruct((part, columns), f32)
    arrays = [(tokens, 1), (tokens, groups - 1), weight]
    return by_columns(kernel, [coded, coded, kept, kept], me, arrays, wait_for, groups, columns)


def pass_on(me, keep_up, keep_down, far_up, far_down):
    part, columns = keep_up.shape

    def kernel(me_ref, keep_up_ref, keep_down_ref, far_up_ref, far_down_ref, up_ref, down_ref):
        def columns_step(cols):
            encode(up_ref, cols, keep_up_ref[:, cols] + decode(far_up_ref, cols, part))
            encode(down_ref, cols, keep_down_ref[:, cols] + decode(far_down_ref, cols, part))

        for_columns(columns, columns_step)

    coded = jax.ShapeDtypeStruct((coded_rows(part), columns), i16)
    return call(kernel, [coded] * 2, me, [keep_up, keep_down, far_up, far_down])


def own_sums(me, tokens, weight, near_down, sum_up, near_up, sum_down, groups, wait_for):
    share, columns = tokens.shape[0] // groups, weight.shape[1]
    part = share // 2

    def kernel(me_ref, a_ref, w_ref, near_down_ref, sum_up_ref, near_up_ref, sum_down_ref, out_ref):
        full = dot(a_ref[...], w_ref[...])
        first = decode(near_down_ref, EVERY, part) + decode(sum_up_ref, EVERY, part)
        second = decode(near_up_ref, EVERY, part) + decode(sum_down_ref, EVERY, part)
        encode(out_ref, EVERY, full + jnp.concatenate([first, second]))

    coded = jax.ShapeDtypeStruct((coded_rows(share), columns), i16)
    arrays = [(tokens, 0), weight, near_down, sum_up, near_up, sum_down]
    return by_columns(kernel, [coded], me, arrays, wait_for, groups, columns, LONG)[0]


def low_rank(positions, panels, tokens, groups, ranks):
    sections, listed, _ = panels.shape
    rows, width = tokens.shape
    share = rows // groups
    spans = listed // ranks
    segs = spans // groups
    seg_rows = share // segs

    def kernel(pos_ref, panels_ref, tokens_ref, out_ref, whole, products):
        n = pl.program_id(0)

        @pl.when(n == 0)
        def _():
            for i in range(sections):
                whole[i * LANES : (i + 1) * LANES, :] = panels_ref[i].T

        products[...] = dot(tokens_ref[...], whole[...]).T
        for g in range(segs):
            start = pl.multiple_of(pos_ref[n * segs + g] * ranks, ranks)
            here = slice(g * seg_rows, (g + 1) * seg_rows)
            out_ref[0, :, here] = products[pl.ds(start, ranks), here]

    return pl.pallas_call(
        kernel,
        grid_spec=pltpu.PrefetchScalarGridSpec(
            num_scalar_prefetch=1,
            grid=(groups,),
            in_specs=[
                pl.BlockSpec(panels.shape, lambda n, pos: (0, 0, 0)),
                pl.BlockSpec((share, width), lambda n, pos: (n, 0)),
            ],
            out_specs=pl.BlockSpec((1, ranks, share), lambda n, pos: (n, 0, 0)),
            scratch_shapes=[pltpu.VMEM((width, listed), bf16), pltpu.VMEM((listed, share), f32)],
        ),
        out_shape=jax.ShapeDtypeStruct((groups, ranks, share), f32),
        cost_estimate=CHEAP,
        compiler_params=pltpu.CompilerParams(vmem_limit_bytes=LARGE),
    )(positions, panels, tokens)


def finish(me, base, arrived, expander):
    pools = len(arrived)
    ranks, share = arrived[0].shape
    segs, full_rank, columns = expander.shape
    seg_rows = share // segs
    halves = 2
    wide = columns // halves

    def kernel(me_ref, base_ref, *refs):
        low_refs, (up_ref, out_ref, low, made, sems) = refs[:pools], refs[pools:]
        for k in range(pools):
            start = pl.multiple_of((me_ref[1] + pools - k) % pools * ranks, ranks)
            low[pl.ds(start, ranks), :] = low_refs[k][...]
        values = low[...].T
        upper = values.astype(bf16)
        lower = (values - upper.astype(f32)).astype(bf16)
        copies = []
        for h in range(halves):
            cols = slice(h * wide, (h + 1) * wide)
            base_values = decode(base_ref, cols, share)
            for g in range(segs):
                here = slice(g * seg_rows, (g + 1) * seg_rows)
                panel = up_ref[g, :, cols]
                correction = dot(upper[here], panel) + dot(lower[here], panel)
                made[h, here, :] = base_values[here] + ADAPTER_SCALE * correction
            copy = pltpu.make_async_copy(made.at[h], out_ref.at[:, cols], sems.at[h])
            copy.start()
            copies.append(copy)
        for copy in copies:
            copy.wait()

    return call(
        kernel,
        jax.ShapeDtypeStruct((share, columns), f32),
        me,
        [base, *arrived, expander],
        out_specs=ANYWHERE,
        scratch_shapes=[
            pltpu.VMEM((pools * ranks, share), f32),
            pltpu.VMEM((halves, share, wide), f32),
            pltpu.SemaphoreType.DMA((halves,)),
        ],
    )


def shards(acts, output_weight, down, up, ids, positions, table):
    sections, groups, pools = (lax.axis_size(a) for a in ("section", "tensor", "pool"))
    me_t, me_p = lax.axis_index("tensor"), lax.axis_index("pool")
    me = jnp.stack([me_t, me_p]).astype(i32)
    slots, ranks, _ = down.shape
    columns = up.shape[2]
    spans = ids.shape[1]
    tokens, weight = acts[0], output_weight[0]
    own_segs = spans // groups
    half = ranks // 2
    marked = slots * (ranks + half)

    spread = spread_pieces(down, up, positions[0])
    held = swap_all(spread, "section")
    hit = ids[:, :, None] == jnp.arange(table.shape[0], dtype=i32)
    slot_ids = jnp.sum(jnp.where(hit, table, 0), axis=-1)

    far_up, far_down = far_sums(me, tokens, weight, groups, [spread])
    near_up, near_down, keep_up, keep_down = near_sums(me, tokens, weight, groups, [far_up])
    far_up, far_down = along(far_up, "tensor", 1), along(far_down, "tensor", -1)
    near_up, near_down = along(near_up, "tensor", 1), along(near_down, "tensor", -1)
    more_up, more_down = pass_on(me, keep_up, keep_down, far_up, far_down)
    sum_up, sum_down = along(more_up, "tensor", 1), along(more_down, "tensor", -1)

    tiles = slot_ids // slots * (held.shape[1] // ranks) + slot_ids % slots
    picked_down = pick_down(held, tiles, ranks, [more_up])
    got_down = swap_all(picked_down, "section")
    base = own_sums(
        me, tokens, weight, near_down, sum_up, near_up, sum_down, groups, [picked_down]
    )
    all_pos = held[:, marked, :spans].astype(i32)
    seg_hit = all_pos[:, :, None] == jnp.arange(spans, dtype=i32)
    seg_slots = jnp.sum(jnp.where(seg_hit, slot_ids[:, None, :], 0), axis=-1)
    picked_up = pick_up(held, jnp.roll(seg_slots, 1, axis=0), slots, ranks, [base])
    base = to_next_section(base, 0)
    got_up = swap_all(
        picked_up.reshape(sections * groups, own_segs * half, LANES), ("section", "tensor")
    )
    expander = (
        got_up.reshape(columns // LANES, 2, groups, own_segs, half, LANES)
        .transpose(3, 2, 1, 4, 0, 5)
        .reshape(own_segs, groups * ranks, columns)
    )

    low = low_rank(positions[0], got_down, tokens, groups, ranks)

    def low_of(distance):
        return lax.dynamic_index_in_dim(low, (me_t + distance) % groups, 0, keepdims=False)

    reduced = low_of(0)
    for distance in range(1, groups):
        reduced = reduced + along(low_of(distance), "tensor", distance)
    arrived = [to_next_section(reduced, k) for k in range(pools)]
    return finish(me, base, arrived, expander)[None]


def solution(mesh):
    return jax.shard_map(
        shards,
        mesh=mesh,
        in_specs=(
            P("section", None, "tensor"),
            P("section", "tensor", "pool"),
            P("section", "pool", "tensor"),
            P("section", "tensor", "pool"),
            P(),
            P("section", None),
            P(),
        ),
        out_specs=P("section", "tensor", "pool"),
        check_vma=False,
    )
```

```python
import functools

import jax
import jax.numpy as jnp
from jax import lax
from jax.experimental import pallas as pl
from jax.experimental.pallas import tpu as pltpu
from jax.sharding import PartitionSpec as P

ADAPTER_SCALE = 2.0
LANES = 128
BLOCK = 16
STEPS = 128.0
TOP = 32767.0
LARGE = 56 * 2**20
COLUMNS = 256
CHEAP = pl.CostEstimate(flops=1000, bytes_accessed=1000, transcendentals=0)
LONG = pl.CostEstimate(flops=50_000_000_000, bytes_accessed=100_000_000, transcendentals=0)
bf16, f32, i16, i32 = jnp.bfloat16, jnp.float32, jnp.int16, jnp.int32


def coded_rows(rows):
    codes = rows // BLOCK
    return rows + (codes + 15) // 16 * 16


def nearest(x):
    return (x + 1.5 * 2.0**23) - 1.5 * 2.0**23


def encode(ref, cols, x):
    rows, width = x.shape
    tail = coded_rows(rows) - rows
    row = lax.broadcasted_iota(i32, (tail, width), 0)
    peaks = jnp.zeros((tail, width), f32)
    for b in range(rows // BLOCK):
        peak = jnp.max(jnp.abs(x[b * BLOCK : (b + 1) * BLOCK]), axis=0, keepdims=True)
        peaks = jnp.where(row == b, peak, peaks)
    codes = jnp.ceil(jnp.log2(jnp.maximum(peaks, 2.0**-110)) * STEPS) + 1.0
    inverse = jnp.exp2(codes * (-1.0 / STEPS)) * TOP
    for b in range(rows // BLOCK):
        part = x[b * BLOCK : (b + 1) * BLOCK] * inverse[b : b + 1]
        ref[b * BLOCK : (b + 1) * BLOCK, cols] = nearest(part).astype(i32).astype(i16)
    ref[rows:, cols] = codes.astype(i32).astype(i16)


def decode(ref, cols, rows):
    codes = ref[rows:, cols].astype(i32).astype(f32)
    scale = jnp.exp2(codes * (1.0 / STEPS)) * (1.0 / TOP)
    parts = []
    for b in range(rows // BLOCK):
        values = ref[b * BLOCK : (b + 1) * BLOCK, cols].astype(i32).astype(f32)
        parts.append(values * scale[b : b + 1])
    return jnp.concatenate(parts)


def along(block, axis, distance):
    n = lax.axis_size(axis)
    return lax.ppermute(block, axis, [(i, (i + distance) % n) for i in range(n)])


def to_next_section(block, pool_distance):
    axes = ("section", "tensor", "pool")
    sections, tensors, pools = (lax.axis_size(a) for a in axes)
    route = [
        (
            (s * tensors + t) * pools + p,
            ((s + 1) % sections * tensors + t) * pools + (p + pool_distance) % pools,
        )
        for s in range(sections)
        for t in range(tensors)
        for p in range(pools)
    ]
    return lax.ppermute(block, axes, route)


def swap_all(block, axis):
    return lax.all_to_all(block, axis, split_axis=0, concat_axis=0, tiled=True)


SCALARS = pl.BlockSpec(memory_space=pltpu.SMEM)
ARRAY = pl.BlockSpec(memory_space=pltpu.VMEM)
ANYWHERE = pl.BlockSpec(memory_space=pl.ANY)
HBM = pl.BlockSpec(memory_space=pltpu.HBM)


def call(
    kernel,
    out_shape,
    scalars,
    arrays,
    wait_for=(),
    in_specs=None,
    out_specs=None,
    scratch_shapes=(),
    vmem=8 * 2**20,
):
    lead = [] if scalars is None else [scalars]
    first, waits = len(lead) + len(arrays), len(wait_for)

    def body(*refs):
        kernel(*refs[:first], *refs[first + waits :])

    many = isinstance(out_shape, list)
    return pl.pallas_call(
        body,
        out_shape=out_shape,
        in_specs=[SCALARS] * len(lead) + (in_specs or [ARRAY] * len(arrays)) + [ANYWHERE] * waits,
        out_specs=out_specs or ([ARRAY] * len(out_shape) if many else ARRAY),
        scratch_shapes=list(scratch_shapes),
        cost_estimate=CHEAP,
        compiler_params=pltpu.CompilerParams(vmem_limit_bytes=vmem),
    )(*lead, *arrays, *wait_for)


def for_columns(columns, body):
    def step(n, carry):
        body(pl.ds(pl.multiple_of(n * COLUMNS, COLUMNS), COLUMNS))
        return carry

    lax.fori_loop(0, columns // COLUMNS, step, 0)


def spread_pieces(down, up, positions):
    slots, ranks, width = down.shape
    columns = up.shape[2]
    half = ranks // 2
    n_down, n_up = slots * ranks, slots * half
    tiles = columns // LANES
    spans = positions.shape[1]
    chunks = 4
    each = 2 * tiles // chunks

    def kernel(pos_hbm, down_hbm, up_hbm, out_hbm, pos_ref, down_ref, up_ref, out_ref, sems, outs):
        gets = []
        for c in range(chunks):
            here = pl.ds(c * each * LANES, each * LANES)
            gets.append(
                pltpu.make_async_copy(down_hbm.at[:, here], down_ref.at[:, here], sems.at[c])
            )
        gets.append(pltpu.make_async_copy(up_hbm, up_ref, sems.at[chunks]))
        gets.append(pltpu.make_async_copy(pos_hbm, pos_ref, sems.at[chunks + 1]))
        for get in gets:
            get.start()
        puts = []
        for c in range(chunks):
            gets[c].wait()
            for i in range(c * each, (c + 1) * each):
                piece = down_ref.at[:, pl.ds(i * LANES, LANES)]
                puts.append(
                    pltpu.make_async_copy(piece, out_hbm.at[i, pl.ds(0, n_down)], outs.at[i])
                )
                puts[i].start()
        gets[chunks].wait()
        gets[chunks + 1].wait()
        lane = lax.broadcasted_iota(i32, (16, LANES), 1)
        marks = jnp.zeros((16, LANES), i32)
        for j in range(spans):
            marks = jnp.where(lane == j, pos_ref[:, j : j + 1], marks)
        marks = marks.astype(f32).astype(bf16)
        for c in range(tiles):
            raised = up_ref[:, :, c * LANES : (c + 1) * LANES].astype(f32)
            for h in range(2):
                piece = raised[:, h * half : (h + 1) * half, :].reshape(n_up, LANES)
                out_ref[2 * c + h, :n_up, :] = piece.astype(bf16)
                out_ref[2 * c + h, n_up:, :] = marks
        rest = pltpu.make_async_copy(
            out_ref, out_hbm.at[:, pl.ds(n_down, n_up + 16)], sems.at[chunks + 2]
        )
        rest.start()
        for put in puts:
            put.wait()
        rest.wait()

    return call(
        kernel,
        jax.ShapeDtypeStruct((2 * tiles, n_down + n_up + 16, LANES), bf16),
        None,
        [positions, down.reshape(n_down, width), up],
        vmem=LARGE,
        in_specs=[HBM] * 3,
        out_specs=HBM,
        scratch_shapes=[
            pltpu.VMEM(positions.shape, i32),
            pltpu.VMEM((n_down, width), bf16),
            pltpu.VMEM(up.shape, bf16),
            pltpu.VMEM((2 * tiles, n_up + 16, LANES), bf16),
            pltpu.SemaphoreType.DMA((chunks + 3,)),
            pltpu.SemaphoreType.DMA((2 * tiles,)),
        ],
    )


def pick_down(held, tiles, ranks, wait_for):
    sections, total, _ = held.shape
    spans = tiles.shape[1]

    def kernel(tiles_ref, held_ref, out_ref):
        for r in range(sections):
            row = [held_ref[tiles_ref[r * spans + j]] for j in range(spans)]
            for j in range(spans):
                out_ref[r, j] = row[j]

    out = jax.ShapeDtypeStruct((sections, spans, ranks, LANES), bf16)
    split = held.reshape(sections * total // ranks, ranks, LANES)
    picked = call(kernel, out, tiles.reshape(-1), [split], wait_for)
    return picked.reshape(sections, spans * ranks, LANES)


def pick_up(held, seg_slots, slots, ranks, wait_for):
    sections, total, _ = held.shape
    spans = seg_slots.shape[1]
    half = ranks // 2
    first, count = slots * ranks, slots * half

    def kernel(ids_ref, held_ref, out_ref, wide):
        for o in range(sections):
            piece = held_ref[o, first : first + count, :].astype(f32)
            wide[o * slots : (o + 1) * slots] = piece.reshape(slots, half, LANES)
        for r in range(sections):
            row = [wide[ids_ref[r * spans + g]] for g in range(spans)]
            out_ref[r] = jnp.concatenate(row).astype(bf16)

    out = jax.ShapeDtypeStruct((sections, spans * half, LANES), bf16)
    wide = pltpu.VMEM((sections * slots, half, LANES), f32)
    return call(kernel, out, seg_slots.reshape(-1), [held], wait_for, scratch_shapes=[wide])


def dot(a, b):
    return jnp.dot(a, b, preferred_element_type=f32)


def by_columns(kernel, outs, me, arrays, wait_for, groups, columns, cost=CHEAP):
    waits = len(wait_for)

    def body(me_ref, *refs):
        kernel(me_ref, *refs[waits:])

    def rows_spec(tokens, distance):
        share = tokens.shape[0] // groups
        return pl.BlockSpec(
            (share, tokens.shape[1]), lambda n, me: ((me[0] + distance) % groups, 0)
        )

    def column_spec(array):
        return pl.BlockSpec((array.shape[0], COLUMNS), lambda n, me: (0, n))

    specs = [rows_spec(*x) if isinstance(x, tuple) else column_spec(x) for x in arrays]
    arrays = [x[0] if isinstance(x, tuple) else x for x in arrays]
    return pl.pallas_call(
        body,
        grid_spec=pltpu.PrefetchScalarGridSpec(
            num_scalar_prefetch=1,
            grid=(columns // COLUMNS,),
            in_specs=[ANYWHERE] * waits + specs,
            out_specs=[column_spec(x) for x in outs],
        ),
        out_shape=outs,
        cost_estimate=cost,
        compiler_params=pltpu.CompilerParams(vmem_limit_bytes=LARGE),
    )(me, *wait_for, *arrays)


EVERY = slice(None)


def far_sums(me, tokens, weight, groups, wait_for):
    part, columns = tokens.shape[0] // groups // 2, weight.shape[1]

    def kernel(me_ref, a_ref, w_ref, up_ref, down_ref):
        full = dot(a_ref[...], w_ref[...])
        encode(up_ref, EVERY, full[:part])
        encode(down_ref, EVERY, full[part:])

    coded = jax.ShapeDtypeStruct((coded_rows(part), columns), i16)
    arrays = [(tokens, 2), weight]
    return by_columns(kernel, [coded] * 2, me, arrays, wait_for, groups, columns)


def near_sums(me, tokens, weight, groups, wait_for):
    part, columns = tokens.shape[0] // groups // 2, weight.shape[1]

    def kernel(me_ref, a_up_ref, a_down_ref, w_ref, up_ref, down_ref, keep_up_ref, keep_down_ref):
        full = dot(a_up_ref[...], w_ref[...])
        keep_up_ref[...] = full[:part]
        encode(up_ref, EVERY, full[part:])
        full = dot(a_down_ref[...], w_ref[...])
        keep_down_ref[...] = full[part:]
        encode(down_ref, EVERY, full[:part])

    coded = jax.ShapeDtypeStruct((coded_rows(part), columns), i16)
    kept = jax.ShapeDtypeStruct((part, columns), f32)
    arrays = [(tokens, 1), (tokens, groups - 1), weight]
    return by_columns(kernel, [coded, coded, kept, kept], me, arrays, wait_for, groups, columns)


def pass_on(me, keep_up, keep_down, far_up, far_down):
    part, columns = keep_up.shape

    def kernel(me_ref, keep_up_ref, keep_down_ref, far_up_ref, far_down_ref, up_ref, down_ref):
        def columns_step(cols):
            encode(up_ref, cols, keep_up_ref[:, cols] + decode(far_up_ref, cols, part))
            encode(down_ref, cols, keep_down_ref[:, cols] + decode(far_down_ref, cols, part))

        for_columns(columns, columns_step)

    coded = jax.ShapeDtypeStruct((coded_rows(part), columns), i16)
    return call(kernel, [coded] * 2, me, [keep_up, keep_down, far_up, far_down])


def own_sums(me, tokens, weight, near_down, sum_up, near_up, sum_down, groups, wait_for):
    share, columns = tokens.shape[0] // groups, weight.shape[1]
    part = share // 2

    def kernel(me_ref, a_ref, w_ref, near_down_ref, sum_up_ref, near_up_ref, sum_down_ref, out_ref):
        full = dot(a_ref[...], w_ref[...])
        first = decode(near_down_ref, EVERY, part) + decode(sum_up_ref, EVERY, part)
        second = decode(near_up_ref, EVERY, part) + decode(sum_down_ref, EVERY, part)
        encode(out_ref, EVERY, full + jnp.concatenate([first, second]))

    coded = jax.ShapeDtypeStruct((coded_rows(share), columns), i16)
    arrays = [(tokens, 0), weight, near_down, sum_up, near_up, sum_down]
    return by_columns(kernel, [coded], me, arrays, wait_for, groups, columns, LONG)[0]


def low_rank(me, panels, tokens, groups, ranks):
    sections, listed, _ = panels.shape
    rows, width = tokens.shape
    share = rows // groups
    spans = listed // ranks
    segs = spans // groups
    seg_rows = share // segs

    def kernel(scalars_ref, panels_ref, tokens_ref, *refs):
        outs, (whole, products) = refs[:groups], refs[groups:]
        for i in range(sections):
            whole[:, i * LANES : (i + 1) * LANES] = panels_ref[i]
        for d in range(groups):
            share_of = (scalars_ref[0] + d) % groups
            rows_here = pl.ds(pl.multiple_of(share_of * share, share), share)
            products[d] = lax.dot_general(
                whole[...],
                tokens_ref[rows_here, :],
                (((1,), (1,)), ((), ())),
                preferred_element_type=f32,
            )
            for g in range(segs):
                listed_at = scalars_ref[2 + share_of * segs + g]
                start = pl.multiple_of(listed_at * ranks, ranks)
                here = slice(g * seg_rows, (g + 1) * seg_rows)
                outs[d][:, here] = products[d, pl.ds(start, ranks), here]

    return call(
        kernel,
        [jax.ShapeDtypeStruct((ranks, share), f32)] * groups,
        me,
        [panels, tokens],
        scratch_shapes=[
            pltpu.VMEM((listed, width), bf16),
            pltpu.VMEM((groups, listed, share), f32),
        ],
    )


def finish(me, base, arrived, expander):
    pools = len(arrived)
    ranks, share = arrived[0].shape
    segs, full_rank, columns = expander.shape
    seg_rows = share // segs
    halves = 2
    wide = columns // halves

    def kernel(me_ref, base_ref, *refs):
        low_refs, (up_ref, out_ref, low, made, sems) = refs[:pools], refs[pools:]
        for k in range(pools):
            start = pl.multiple_of((me_ref[1] + pools - k) % pools * ranks, ranks)
            low[pl.ds(start, ranks), :] = low_refs[k][...]
        values = low[...].T
        upper = values.astype(bf16)
        lower = (values - upper.astype(f32)).astype(bf16)
        copies = []
        for h in range(halves):
            cols = slice(h * wide, (h + 1) * wide)
            base_values = decode(base_ref, cols, share)
            for g in range(segs):
                here = slice(g * seg_rows, (g + 1) * seg_rows)
                panel = up_ref[g, :, cols]
                correction = dot(upper[here], panel) + dot(lower[here], panel)
                made[h, here, :] = base_values[here] + ADAPTER_SCALE * correction
            copy = pltpu.make_async_copy(made.at[h], out_ref.at[:, cols], sems.at[h])
            copy.start()
            copies.append(copy)
        for copy in copies:
            copy.wait()

    return call(
        kernel,
        jax.ShapeDtypeStruct((share, columns), f32),
        me,
        [base, *arrived, expander],
        out_specs=ANYWHERE,
        scratch_shapes=[
            pltpu.VMEM((pools * ranks, share), f32),
            pltpu.VMEM((halves, share, wide), f32),
            pltpu.SemaphoreType.DMA((halves,)),
        ],
    )


def shards(acts, output_weight, down, up, ids, positions, table):
    sections, groups, pools = (lax.axis_size(a) for a in ("section", "tensor", "pool"))
    me_t, me_p = lax.axis_index("tensor"), lax.axis_index("pool")
    me = jnp.concatenate([jnp.stack([me_t, me_p]).astype(i32), positions[0]])
    slots, ranks, _ = down.shape
    columns = up.shape[2]
    spans = ids.shape[1]
    tokens, weight = acts[0], output_weight[0]
    own_segs = spans // groups
    half = ranks // 2
    marked = slots * (ranks + half)

    spread = spread_pieces(down, up, positions)
    held = swap_all(spread, "section")
    hit = ids[:, :, None] == jnp.arange(table.shape[0], dtype=i32)
    slot_ids = jnp.sum(jnp.where(hit, table, 0), axis=-1)

    far_up, far_down = far_sums(me, tokens, weight, groups, [spread])
    near_up, near_down, keep_up, keep_down = near_sums(me, tokens, weight, groups, [far_up])
    far_up, far_down = along(far_up, "tensor", 1), along(far_down, "tensor", -1)
    near_up, near_down = along(near_up, "tensor", 1), along(near_down, "tensor", -1)
    more_up, more_down = pass_on(me, keep_up, keep_down, far_up, far_down)
    sum_up, sum_down = along(more_up, "tensor", 1), along(more_down, "tensor", -1)

    tiles = slot_ids // slots * (held.shape[1] // ranks) + slot_ids % slots
    picked_down = pick_down(held, tiles, ranks, [more_up])
    got_down = swap_all(picked_down, "section")
    base = own_sums(
        me, tokens, weight, near_down, sum_up, near_up, sum_down, groups, [picked_down]
    )
    all_pos = held[:, marked, :spans].astype(i32)
    seg_hit = all_pos[:, :, None] == jnp.arange(spans, dtype=i32)
    seg_slots = jnp.sum(jnp.where(seg_hit, slot_ids[:, None, :], 0), axis=-1)
    picked_up = pick_up(held, jnp.roll(seg_slots, 1, axis=0), slots, ranks, [base])
    base = to_next_section(base, 0)
    got_up = swap_all(
        picked_up.reshape(sections * groups, own_segs * half, LANES), ("section", "tensor")
    )
    expander = (
        got_up.reshape(columns // LANES, 2, groups, own_segs, half, LANES)
        .transpose(3, 2, 1, 4, 0, 5)
        .reshape(own_segs, groups * ranks, columns)
    )

    low = low_rank(me, got_down, tokens, groups, ranks)
    reduced = low[0]
    for distance in range(1, groups):
        reduced = reduced + along(low[distance], "tensor", distance)
    arrived = [to_next_section(reduced, k) for k in range(pools)]
    return finish(me, base, arrived, expander)[None]


def solution(mesh):
    return jax.shard_map(
        shards,
        mesh=mesh,
        in_specs=(
            P("section", None, "tensor"),
            P("section", "tensor", "pool"),
            P("section", "pool", "tensor"),
            P("section", "tensor", "pool"),
            P(),
            P("section", None),
            P(),
        ),
        out_specs=P("section", "tensor", "pool"),
        check_vma=False,
    )
```

```python
import functools

import jax
import jax.numpy as jnp
from jax import lax
from jax.experimental import pallas as pl
from jax.experimental.pallas import tpu as pltpu
from jax.sharding import PartitionSpec as P

ADAPTER_SCALE = 2.0
LANES = 128
BLOCK = 16
STEPS = 128.0
TOP = 32767.0
LARGE = 56 * 2**20
COLUMNS = 256
CHEAP = pl.CostEstimate(flops=1000, bytes_accessed=1000, transcendentals=0)
LONG = pl.CostEstimate(flops=50_000_000_000, bytes_accessed=100_000_000, transcendentals=0)
bf16, f32, i16, i32 = jnp.bfloat16, jnp.float32, jnp.int16, jnp.int32


def coded_rows(rows):
    codes = rows // BLOCK
    return rows + (codes + 15) // 16 * 16


def nearest(x):
    return (x + 1.5 * 2.0**23) - 1.5 * 2.0**23


def encode(ref, cols, x):
    rows, width = x.shape
    tail = coded_rows(rows) - rows
    row = lax.broadcasted_iota(i32, (tail, width), 0)
    peaks = jnp.zeros((tail, width), f32)
    for b in range(rows // BLOCK):
        peak = jnp.max(jnp.abs(x[b * BLOCK : (b + 1) * BLOCK]), axis=0, keepdims=True)
        peaks = jnp.where(row == b, peak, peaks)
    codes = jnp.ceil(jnp.log2(jnp.maximum(peaks, 2.0**-110)) * STEPS) + 1.0
    inverse = jnp.exp2(codes * (-1.0 / STEPS)) * TOP
    for b in range(rows // BLOCK):
        part = x[b * BLOCK : (b + 1) * BLOCK] * inverse[b : b + 1]
        ref[b * BLOCK : (b + 1) * BLOCK, cols] = nearest(part).astype(i32).astype(i16)
    ref[rows:, cols] = codes.astype(i32).astype(i16)


def decode(ref, cols, rows):
    codes = ref[rows:, cols].astype(i32).astype(f32)
    scale = jnp.exp2(codes * (1.0 / STEPS)) * (1.0 / TOP)
    parts = []
    for b in range(rows // BLOCK):
        values = ref[b * BLOCK : (b + 1) * BLOCK, cols].astype(i32).astype(f32)
        parts.append(values * scale[b : b + 1])
    return jnp.concatenate(parts)


def along(block, axis, distance):
    n = lax.axis_size(axis)
    return lax.ppermute(block, axis, [(i, (i + distance) % n) for i in range(n)])


def to_next_section(block, pool_distance):
    axes = ("section", "tensor", "pool")
    sections, tensors, pools = (lax.axis_size(a) for a in axes)
    route = [
        (
            (s * tensors + t) * pools + p,
            ((s + 1) % sections * tensors + t) * pools + (p + pool_distance) % pools,
        )
        for s in range(sections)
        for t in range(tensors)
        for p in range(pools)
    ]
    return lax.ppermute(block, axes, route)


def swap_all(block, axis):
    return lax.all_to_all(block, axis, split_axis=0, concat_axis=0, tiled=True)


SCALARS = pl.BlockSpec(memory_space=pltpu.SMEM)
ARRAY = pl.BlockSpec(memory_space=pltpu.VMEM)
ANYWHERE = pl.BlockSpec(memory_space=pl.ANY)
HBM = pl.BlockSpec(memory_space=pltpu.HBM)


def call(
    kernel,
    out_shape,
    scalars,
    arrays,
    wait_for=(),
    in_specs=None,
    out_specs=None,
    scratch_shapes=(),
    vmem=8 * 2**20,
):
    lead = [] if scalars is None else [scalars]
    first, waits = len(lead) + len(arrays), len(wait_for)

    def body(*refs):
        kernel(*refs[:first], *refs[first + waits :])

    many = isinstance(out_shape, list)
    return pl.pallas_call(
        body,
        out_shape=out_shape,
        in_specs=[SCALARS] * len(lead) + (in_specs or [ARRAY] * len(arrays)) + [ANYWHERE] * waits,
        out_specs=out_specs or ([ARRAY] * len(out_shape) if many else ARRAY),
        scratch_shapes=list(scratch_shapes),
        cost_estimate=CHEAP,
        compiler_params=pltpu.CompilerParams(vmem_limit_bytes=vmem),
    )(*lead, *arrays, *wait_for)


def for_columns(columns, body):
    def step(n, carry):
        body(pl.ds(pl.multiple_of(n * COLUMNS, COLUMNS), COLUMNS))
        return carry

    lax.fori_loop(0, columns // COLUMNS, step, 0)


def spread_pieces(down, up, positions):
    slots, ranks, width = down.shape
    columns = up.shape[2]
    half = ranks // 2
    n_down, n_up = slots * ranks, slots * half
    tiles = columns // LANES
    spans = positions.shape[1]
    chunks = 4
    each = 2 * tiles // chunks

    def kernel(pos_hbm, down_hbm, up_hbm, out_hbm, pos_ref, down_ref, up_ref, out_ref, sems, outs):
        gets = []
        for c in range(chunks):
            here = pl.ds(c * each * LANES, each * LANES)
            gets.append(
                pltpu.make_async_copy(down_hbm.at[:, here], down_ref.at[:, here], sems.at[c])
            )
        gets.append(pltpu.make_async_copy(up_hbm, up_ref, sems.at[chunks]))
        gets.append(pltpu.make_async_copy(pos_hbm, pos_ref, sems.at[chunks + 1]))
        for get in gets:
            get.start()
        puts = []
        for c in range(chunks):
            gets[c].wait()
            for i in range(c * each, (c + 1) * each):
                piece = down_ref.at[:, pl.ds(i * LANES, LANES)]
                puts.append(
                    pltpu.make_async_copy(piece, out_hbm.at[i, pl.ds(0, n_down)], outs.at[i])
                )
                puts[i].start()
        gets[chunks].wait()
        gets[chunks + 1].wait()
        lane = lax.broadcasted_iota(i32, (16, LANES), 1)
        marks = jnp.zeros((16, LANES), i32)
        for j in range(spans):
            marks = jnp.where(lane == j, pos_ref[:, j : j + 1], marks)
        marks = marks.astype(f32).astype(bf16)
        for c in range(tiles):
            raised = up_ref[:, :, c * LANES : (c + 1) * LANES].astype(f32)
            for h in range(2):
                piece = raised[:, h * half : (h + 1) * half, :].reshape(n_up, LANES)
                out_ref[2 * c + h, :n_up, :] = piece.astype(bf16)
                out_ref[2 * c + h, n_up:, :] = marks
        rest = pltpu.make_async_copy(
            out_ref, out_hbm.at[:, pl.ds(n_down, n_up + 16)], sems.at[chunks + 2]
        )
        rest.start()
        for put in puts:
            put.wait()
        rest.wait()

    return call(
        kernel,
        jax.ShapeDtypeStruct((2 * tiles, n_down + n_up + 16, LANES), bf16),
        None,
        [positions, down.reshape(n_down, width), up],
        vmem=LARGE,
        in_specs=[HBM] * 3,
        out_specs=HBM,
        scratch_shapes=[
            pltpu.VMEM(positions.shape, i32),
            pltpu.VMEM((n_down, width), bf16),
            pltpu.VMEM(up.shape, bf16),
            pltpu.VMEM((2 * tiles, n_up + 16, LANES), bf16),
            pltpu.SemaphoreType.DMA((chunks + 3,)),
            pltpu.SemaphoreType.DMA((2 * tiles,)),
        ],
    )


def pick_down(held, tiles, ranks, wait_for):
    sections, total, _ = held.shape
    spans = tiles.shape[1]

    def kernel(tiles_ref, held_ref, out_ref):
        for r in range(sections):
            row = [held_ref[tiles_ref[r * spans + j]] for j in range(spans)]
            for j in range(spans):
                out_ref[r, j] = row[j]

    out = jax.ShapeDtypeStruct((sections, spans, ranks, LANES), bf16)
    split = held.reshape(sections * total // ranks, ranks, LANES)
    picked = call(kernel, out, tiles.reshape(-1), [split], wait_for)
    return picked.reshape(sections, spans * ranks, LANES)


def pick_up(held, seg_slots, slots, ranks, wait_for):
    sections, total, _ = held.shape
    spans = seg_slots.shape[1]
    half = ranks // 2
    first, count = slots * ranks, slots * half

    def kernel(ids_ref, held_ref, out_ref, wide):
        for o in range(sections):
            piece = held_ref[o, first : first + count, :].astype(f32)
            wide[o * slots : (o + 1) * slots] = piece.reshape(slots, half, LANES)
        for r in range(sections):
            row = [wide[ids_ref[r * spans + g]] for g in range(spans)]
            out_ref[r] = jnp.concatenate(row).astype(bf16)

    out = jax.ShapeDtypeStruct((sections, spans * half, LANES), bf16)
    wide = pltpu.VMEM((sections * slots, half, LANES), f32)
    return call(kernel, out, seg_slots.reshape(-1), [held], wait_for, scratch_shapes=[wide])


def dot(a, b):
    return jnp.dot(a, b, preferred_element_type=f32)


def by_columns(kernel, outs, me, arrays, wait_for, groups, columns, cost=CHEAP):
    waits = len(wait_for)

    def body(me_ref, *refs):
        kernel(me_ref, *refs[waits:])

    def rows_spec(tokens, distance):
        share = tokens.shape[0] // groups
        return pl.BlockSpec(
            (share, tokens.shape[1]), lambda n, me: ((me[0] + distance) % groups, 0)
        )

    def column_spec(array):
        return pl.BlockSpec((array.shape[0], COLUMNS), lambda n, me: (0, n))

    specs = [rows_spec(*x) if isinstance(x, tuple) else column_spec(x) for x in arrays]
    arrays = [x[0] if isinstance(x, tuple) else x for x in arrays]
    return pl.pallas_call(
        body,
        grid_spec=pltpu.PrefetchScalarGridSpec(
            num_scalar_prefetch=1,
            grid=(columns // COLUMNS,),
            in_specs=[ANYWHERE] * waits + specs,
            out_specs=[column_spec(x) for x in outs],
        ),
        out_shape=outs,
        cost_estimate=cost,
        compiler_params=pltpu.CompilerParams(vmem_limit_bytes=LARGE),
    )(me, *wait_for, *arrays)


EVERY = slice(None)


def far_sums(me, tokens, weight, groups, wait_for):
    part, columns = tokens.shape[0] // groups // 2, weight.shape[1]

    def kernel(me_ref, a_ref, w_ref, up_ref, down_ref):
        full = dot(a_ref[...], w_ref[...])
        encode(up_ref, EVERY, full[:part])
        encode(down_ref, EVERY, full[part:])

    coded = jax.ShapeDtypeStruct((coded_rows(part), columns), i16)
    arrays = [(tokens, 2), weight]
    return by_columns(kernel, [coded] * 2, me, arrays, wait_for, groups, columns)


def near_sums(me, tokens, weight, groups, wait_for):
    part, columns = tokens.shape[0] // groups // 2, weight.shape[1]

    def kernel(me_ref, a_up_ref, a_down_ref, w_ref, up_ref, down_ref, keep_up_ref, keep_down_ref):
        full = dot(a_up_ref[...], w_ref[...])
        keep_up_ref[...] = full[:part]
        encode(up_ref, EVERY, full[part:])
        full = dot(a_down_ref[...], w_ref[...])
        keep_down_ref[...] = full[part:]
        encode(down_ref, EVERY, full[:part])

    coded = jax.ShapeDtypeStruct((coded_rows(part), columns), i16)
    kept = jax.ShapeDtypeStruct((part, columns), f32)
    arrays = [(tokens, 1), (tokens, groups - 1), weight]
    return by_columns(kernel, [coded, coded, kept, kept], me, arrays, wait_for, groups, columns)


def pass_on(me, keep_up, keep_down, far_up, far_down):
    part, columns = keep_up.shape

    def kernel(me_ref, keep_up_ref, keep_down_ref, far_up_ref, far_down_ref, up_ref, down_ref):
        def columns_step(cols):
            encode(up_ref, cols, keep_up_ref[:, cols] + decode(far_up_ref, cols, part))
            encode(down_ref, cols, keep_down_ref[:, cols] + decode(far_down_ref, cols, part))

        for_columns(columns, columns_step)

    coded = jax.ShapeDtypeStruct((coded_rows(part), columns), i16)
    return call(kernel, [coded] * 2, me, [keep_up, keep_down, far_up, far_down])


def own_sums(me, tokens, weight, near_down, sum_up, near_up, sum_down, groups, wait_for):
    share, columns = tokens.shape[0] // groups, weight.shape[1]
    part = share // 2

    def kernel(me_ref, a_ref, w_ref, near_down_ref, sum_up_ref, near_up_ref, sum_down_ref, out_ref):
        full = dot(a_ref[...], w_ref[...])
        first = decode(near_down_ref, EVERY, part) + decode(sum_up_ref, EVERY, part)
        second = decode(near_up_ref, EVERY, part) + decode(sum_down_ref, EVERY, part)
        encode(out_ref, EVERY, full + jnp.concatenate([first, second]))

    coded = jax.ShapeDtypeStruct((coded_rows(share), columns), i16)
    arrays = [(tokens, 0), weight, near_down, sum_up, near_up, sum_down]
    return by_columns(kernel, [coded], me, arrays, wait_for, groups, columns, LONG)[0]


def low_rank(me, panels, tokens, groups, ranks, distances, wait_for=()):
    sections, listed, _ = panels.shape
    rows, width = tokens.shape
    share = rows // groups
    spans = listed // ranks
    segs = spans // groups
    seg_rows = share // segs
    count = len(distances)

    def kernel(scalars_ref, panels_ref, tokens_ref, *refs):
        outs, (whole, products) = refs[:count], refs[count:]
        for i in range(sections):
            whole[:, i * LANES : (i + 1) * LANES] = panels_ref[i]
        for d in range(count):
            share_of = (scalars_ref[0] + distances[d]) % groups
            rows_here = pl.ds(pl.multiple_of(share_of * share, share), share)
            products[d] = lax.dot_general(
                whole[...],
                tokens_ref[rows_here, :],
                (((1,), (1,)), ((), ())),
                preferred_element_type=f32,
            )
            for g in range(segs):
                listed_at = scalars_ref[2 + share_of * segs + g]
                start = pl.multiple_of(listed_at * ranks, ranks)
                here = slice(g * seg_rows, (g + 1) * seg_rows)
                outs[d][:, here] = products[d, pl.ds(start, ranks), here]

    return call(
        kernel,
        [jax.ShapeDtypeStruct((ranks, share), f32)] * count,
        me,
        [panels, tokens],
        wait_for,
        scratch_shapes=[
            pltpu.VMEM((listed, width), bf16),
            pltpu.VMEM((count, listed, share), f32),
        ],
    )


def finish(me, base, arrived, expander):
    pools = len(arrived)
    ranks, share = arrived[0].shape
    segs, full_rank, columns = expander.shape
    seg_rows = share // segs
    halves = 2
    wide = columns // halves

    def kernel(me_ref, base_ref, *refs):
        low_refs, (up_ref, out_ref, low, made, sems) = refs[:pools], refs[pools:]
        for k in range(pools):
            start = pl.multiple_of((me_ref[1] + pools - k) % pools * ranks, ranks)
            low[pl.ds(start, ranks), :] = low_refs[k][...]
        values = low[...].T
        upper = values.astype(bf16)
        lower = (values - upper.astype(f32)).astype(bf16)
        copies = []
        for h in range(halves):
            cols = slice(h * wide, (h + 1) * wide)
            base_values = decode(base_ref, cols, share)
            for g in range(segs):
                here = slice(g * seg_rows, (g + 1) * seg_rows)
                panel = up_ref[g, :, cols]
                correction = dot(upper[here], panel) + dot(lower[here], panel)
                made[h, here, :] = base_values[here] + ADAPTER_SCALE * correction
            copy = pltpu.make_async_copy(made.at[h], out_ref.at[:, cols], sems.at[h])
            copy.start()
            copies.append(copy)
        for copy in copies:
            copy.wait()

    return call(
        kernel,
        jax.ShapeDtypeStruct((share, columns), f32),
        me,
        [base, *arrived, expander],
        out_specs=ANYWHERE,
        scratch_shapes=[
            pltpu.VMEM((pools * ranks, share), f32),
            pltpu.VMEM((halves, share, wide), f32),
            pltpu.SemaphoreType.DMA((halves,)),
        ],
    )


def shards(acts, output_weight, down, up, ids, positions, table):
    sections, groups, pools = (lax.axis_size(a) for a in ("section", "tensor", "pool"))
    me_t, me_p = lax.axis_index("tensor"), lax.axis_index("pool")
    me = jnp.concatenate([jnp.stack([me_t, me_p]).astype(i32), positions[0]])
    slots, ranks, _ = down.shape
    columns = up.shape[2]
    spans = ids.shape[1]
    tokens, weight = acts[0], output_weight[0]
    own_segs = spans // groups
    half = ranks // 2
    marked = slots * (ranks + half)

    spread = spread_pieces(down, up, positions)
    held = swap_all(spread, "section")
    hit = ids[:, :, None] == jnp.arange(table.shape[0], dtype=i32)
    slot_ids = jnp.sum(jnp.where(hit, table, 0), axis=-1)

    far_up, far_down = far_sums(me, tokens, weight, groups, [spread])
    near_up, near_down, keep_up, keep_down = near_sums(me, tokens, weight, groups, [far_up])
    far_up, far_down = along(far_up, "tensor", 1), along(far_down, "tensor", -1)
    near_up, near_down = along(near_up, "tensor", 1), along(near_down, "tensor", -1)
    more_up, more_down = pass_on(me, keep_up, keep_down, far_up, far_down)
    sum_up, sum_down = along(more_up, "tensor", 1), along(more_down, "tensor", -1)

    tiles = slot_ids // slots * (held.shape[1] // ranks) + slot_ids % slots
    picked_down = pick_down(held, tiles, ranks, [more_up])
    got_down = swap_all(picked_down, "section")
    base = own_sums(
        me, tokens, weight, near_down, sum_up, near_up, sum_down, groups, [picked_down]
    )
    all_pos = held[:, marked, :spans].astype(i32)
    seg_hit = all_pos[:, :, None] == jnp.arange(spans, dtype=i32)
    seg_slots = jnp.sum(jnp.where(seg_hit, slot_ids[:, None, :], 0), axis=-1)
    picked_up = pick_up(held, jnp.roll(seg_slots, 1, axis=0), slots, ranks, [base])
    base = to_next_section(base, 0)
    got_up = swap_all(
        picked_up.reshape(sections * groups, own_segs * half, LANES), ("section", "tensor")
    )
    expander = (
        got_up.reshape(columns // LANES, 2, groups, own_segs, half, LANES)
        .transpose(3, 2, 1, 4, 0, 5)
        .reshape(own_segs, groups * ranks, columns)
    )

    others = list(range(1, groups))
    sent = low_rank(me, got_down, tokens, groups, ranks, others)
    (reduced,) = low_rank(me, got_down, tokens, groups, ranks, [0], [sent[0]])
    for distance in others:
        reduced = reduced + along(sent[distance - 1], "tensor", distance)
    arrived = [to_next_section(reduced, k) for k in range(pools)]
    return finish(me, base, arrived, expander)[None]


def solution(mesh):
    return jax.shard_map(
        shards,
        mesh=mesh,
        in_specs=(
            P("section", None, "tensor"),
            P("section", "tensor", "pool"),
            P("section", "pool", "tensor"),
            P("section", "tensor", "pool"),
            P(),
            P("section", None),
            P(),
        ),
        out_specs=P("section", "tensor", "pool"),
        check_vma=False,
    )
```

```python
import functools

import jax
import jax.numpy as jnp
from jax import lax
from jax.experimental import pallas as pl
from jax.experimental.pallas import tpu as pltpu
from jax.sharding import PartitionSpec as P

ADAPTER_SCALE = 2.0
LANES = 128
BLOCK = 16
STEPS = 128.0
TOP = 32767.0
LARGE = 56 * 2**20
COLUMNS = 256
CHEAP = pl.CostEstimate(flops=1000, bytes_accessed=1000, transcendentals=0)
LONG = pl.CostEstimate(flops=50_000_000_000, bytes_accessed=100_000_000, transcendentals=0)
bf16, f32, i16, i32 = jnp.bfloat16, jnp.float32, jnp.int16, jnp.int32


def coded_rows(rows):
    codes = rows // BLOCK
    return rows + (codes + 15) // 16 * 16


def nearest(x):
    return (x + 1.5 * 2.0**23) - 1.5 * 2.0**23


def encode(ref, cols, x):
    rows, width = x.shape
    tail = coded_rows(rows) - rows
    row = lax.broadcasted_iota(i32, (tail, width), 0)
    peaks = jnp.zeros((tail, width), f32)
    for b in range(rows // BLOCK):
        peak = jnp.max(jnp.abs(x[b * BLOCK : (b + 1) * BLOCK]), axis=0, keepdims=True)
        peaks = jnp.where(row == b, peak, peaks)
    codes = jnp.ceil(jnp.log2(jnp.maximum(peaks, 2.0**-110)) * STEPS) + 1.0
    inverse = jnp.exp2(codes * (-1.0 / STEPS)) * TOP
    for b in range(rows // BLOCK):
        part = x[b * BLOCK : (b + 1) * BLOCK] * inverse[b : b + 1]
        ref[b * BLOCK : (b + 1) * BLOCK, cols] = nearest(part).astype(i32).astype(i16)
    ref[rows:, cols] = codes.astype(i32).astype(i16)


def decode(ref, cols, rows):
    codes = ref[rows:, cols].astype(i32).astype(f32)
    scale = jnp.exp2(codes * (1.0 / STEPS)) * (1.0 / TOP)
    parts = []
    for b in range(rows // BLOCK):
        values = ref[b * BLOCK : (b + 1) * BLOCK, cols].astype(i32).astype(f32)
        parts.append(values * scale[b : b + 1])
    return jnp.concatenate(parts)


def along(block, axis, distance):
    n = lax.axis_size(axis)
    return lax.ppermute(block, axis, [(i, (i + distance) % n) for i in range(n)])


def to_next_section(block, pool_distance):
    axes = ("section", "tensor", "pool")
    sections, tensors, pools = (lax.axis_size(a) for a in axes)
    route = [
        (
            (s * tensors + t) * pools + p,
            ((s + 1) % sections * tensors + t) * pools + (p + pool_distance) % pools,
        )
        for s in range(sections)
        for t in range(tensors)
        for p in range(pools)
    ]
    return lax.ppermute(block, axes, route)


def swap_all(block, axis):
    return lax.all_to_all(block, axis, split_axis=0, concat_axis=0, tiled=True)


SCALARS = pl.BlockSpec(memory_space=pltpu.SMEM)
ARRAY = pl.BlockSpec(memory_space=pltpu.VMEM)
ANYWHERE = pl.BlockSpec(memory_space=pl.ANY)
HBM = pl.BlockSpec(memory_space=pltpu.HBM)


def call(
    kernel,
    out_shape,
    scalars,
    arrays,
    wait_for=(),
    in_specs=None,
    out_specs=None,
    scratch_shapes=(),
    vmem=8 * 2**20,
):
    lead = [] if scalars is None else [scalars]
    first, waits = len(lead) + len(arrays), len(wait_for)

    def body(*refs):
        kernel(*refs[:first], *refs[first + waits :])

    many = isinstance(out_shape, list)
    return pl.pallas_call(
        body,
        out_shape=out_shape,
        in_specs=[SCALARS] * len(lead) + (in_specs or [ARRAY] * len(arrays)) + [ANYWHERE] * waits,
        out_specs=out_specs or ([ARRAY] * len(out_shape) if many else ARRAY),
        scratch_shapes=list(scratch_shapes),
        cost_estimate=CHEAP,
        compiler_params=pltpu.CompilerParams(vmem_limit_bytes=vmem),
    )(*lead, *arrays, *wait_for)


def for_columns(columns, body):
    def step(n, carry):
        body(pl.ds(pl.multiple_of(n * COLUMNS, COLUMNS), COLUMNS))
        return carry

    lax.fori_loop(0, columns // COLUMNS, step, 0)


def spread_pieces(down, up, positions):
    slots, ranks, width = down.shape
    columns = up.shape[2]
    half = ranks // 2
    n_down, n_up = slots * ranks, slots * half
    tiles = columns // LANES
    spans = positions.shape[1]
    chunks = 4
    each = 2 * tiles // chunks

    def kernel(pos_hbm, down_hbm, up_hbm, out_hbm, pos_ref, down_ref, up_ref, out_ref, sems, outs):
        gets = []
        for c in range(chunks):
            here = pl.ds(c * each * LANES, each * LANES)
            gets.append(
                pltpu.make_async_copy(down_hbm.at[:, here], down_ref.at[:, here], sems.at[c])
            )
        gets.append(pltpu.make_async_copy(up_hbm, up_ref, sems.at[chunks]))
        gets.append(pltpu.make_async_copy(pos_hbm, pos_ref, sems.at[chunks + 1]))
        for get in gets:
            get.start()
        puts = []
        for c in range(chunks):
            gets[c].wait()
            for i in range(c * each, (c + 1) * each):
                piece = down_ref.at[:, pl.ds(i * LANES, LANES)]
                puts.append(
                    pltpu.make_async_copy(piece, out_hbm.at[i, pl.ds(0, n_down)], outs.at[i])
                )
                puts[i].start()
        gets[chunks].wait()
        gets[chunks + 1].wait()
        lane = lax.broadcasted_iota(i32, (8, LANES), 1)
        marks = jnp.zeros((8, LANES), i32)
        for j in range(spans):
            marks = jnp.where(lane == j, pos_ref[:, j : j + 1], marks)
        marks = marks.astype(f32).astype(bf16)
        for c in range(tiles):
            raised = up_ref[:, :, c * LANES : (c + 1) * LANES].astype(f32)
            for h in range(2):
                piece = raised[:, h * half : (h + 1) * half, :].reshape(n_up, LANES)
                out_ref[2 * c + h, :n_up, :] = piece.astype(bf16)
                out_ref[2 * c + h, n_up:, :] = marks
        rest = pltpu.make_async_copy(
            out_ref, out_hbm.at[:, pl.ds(n_down, n_up + 8)], sems.at[chunks + 2]
        )
        rest.start()
        for put in puts:
            put.wait()
        rest.wait()

    return call(
        kernel,
        jax.ShapeDtypeStruct((2 * tiles, n_down + n_up + 8, LANES), bf16),
        None,
        [positions, down.reshape(n_down, width), up],
        vmem=LARGE,
        in_specs=[HBM] * 3,
        out_specs=HBM,
        scratch_shapes=[
            pltpu.VMEM(positions.shape, i32),
            pltpu.VMEM((n_down, width), bf16),
            pltpu.VMEM(up.shape, bf16),
            pltpu.VMEM((2 * tiles, n_up + 8, LANES), bf16),
            pltpu.SemaphoreType.DMA((chunks + 3,)),
            pltpu.SemaphoreType.DMA((2 * tiles,)),
        ],
    )


def pick_down(held, owners, starts, ranks, wait_for):
    sections, _, _ = held.shape
    spans = owners.shape[1]
    count = sections * spans

    def kernel(scalars_ref, held_ref, out_ref):
        for r in range(sections):
            row = []
            for n in range(r * spans, (r + 1) * spans):
                start = pl.multiple_of(scalars_ref[count + n], ranks)
                row.append(held_ref[scalars_ref[n], pl.ds(start, ranks), :])
            for j in range(spans):
                out_ref[r, j] = row[j]

    out = jax.ShapeDtypeStruct((sections, spans, ranks, LANES), bf16)
    scalars = jnp.concatenate([owners.reshape(-1), starts.reshape(-1)])
    picked = call(kernel, out, scalars, [held], wait_for)
    return picked.reshape(sections, spans * ranks, LANES)


def pick_up(held, seg_slots, slots, ranks, wait_for):
    sections, total, _ = held.shape
    spans = seg_slots.shape[1]
    half = ranks // 2
    first, count = slots * ranks, slots * half

    def kernel(ids_ref, held_ref, out_ref, wide):
        for o in range(sections):
            piece = held_ref[o, first : first + count, :].astype(f32)
            wide[o * slots : (o + 1) * slots] = piece.reshape(slots, half, LANES)
        for r in range(sections):
            row = [wide[ids_ref[r * spans + g]] for g in range(spans)]
            out_ref[r] = jnp.concatenate(row).astype(bf16)

    out = jax.ShapeDtypeStruct((sections, spans * half, LANES), bf16)
    wide = pltpu.VMEM((sections * slots, half, LANES), f32)
    return call(kernel, out, seg_slots.reshape(-1), [held], wait_for, scratch_shapes=[wide])


def dot(a, b):
    return jnp.dot(a, b, preferred_element_type=f32)


def by_columns(kernel, outs, me, arrays, wait_for, groups, columns, cost=CHEAP):
    waits = len(wait_for)

    def body(me_ref, *refs):
        kernel(me_ref, *refs[waits:])

    def rows_spec(tokens, distance):
        share = tokens.shape[0] // groups
        return pl.BlockSpec(
            (share, tokens.shape[1]), lambda n, me: ((me[0] + distance) % groups, 0)
        )

    def column_spec(array):
        return pl.BlockSpec((array.shape[0], COLUMNS), lambda n, me: (0, n))

    specs = [rows_spec(*x) if isinstance(x, tuple) else column_spec(x) for x in arrays]
    arrays = [x[0] if isinstance(x, tuple) else x for x in arrays]
    return pl.pallas_call(
        body,
        grid_spec=pltpu.PrefetchScalarGridSpec(
            num_scalar_prefetch=1,
            grid=(columns // COLUMNS,),
            in_specs=[ANYWHERE] * waits + specs,
            out_specs=[column_spec(x) for x in outs],
        ),
        out_shape=outs,
        cost_estimate=cost,
        compiler_params=pltpu.CompilerParams(vmem_limit_bytes=LARGE),
    )(me, *wait_for, *arrays)


EVERY = slice(None)


def far_sums(me, tokens, weight, groups, wait_for):
    part, columns = tokens.shape[0] // groups // 2, weight.shape[1]

    def kernel(me_ref, a_ref, w_ref, up_ref, down_ref):
        full = dot(a_ref[...], w_ref[...])
        encode(up_ref, EVERY, full[:part])
        encode(down_ref, EVERY, full[part:])

    coded = jax.ShapeDtypeStruct((coded_rows(part), columns), i16)
    arrays = [(tokens, 2), weight]
    return by_columns(kernel, [coded] * 2, me, arrays, wait_for, groups, columns)


def near_sums(me, tokens, weight, groups, wait_for):
    part, columns = tokens.shape[0] // groups // 2, weight.shape[1]

    def kernel(me_ref, a_up_ref, a_down_ref, w_ref, up_ref, down_ref, keep_up_ref, keep_down_ref):
        full = dot(a_up_ref[...], w_ref[...])
        keep_up_ref[...] = full[:part]
        encode(up_ref, EVERY, full[part:])
        full = dot(a_down_ref[...], w_ref[...])
        keep_down_ref[...] = full[part:]
        encode(down_ref, EVERY, full[:part])

    coded = jax.ShapeDtypeStruct((coded_rows(part), columns), i16)
    kept = jax.ShapeDtypeStruct((part, columns), f32)
    arrays = [(tokens, 1), (tokens, groups - 1), weight]
    return by_columns(kernel, [coded, coded, kept, kept], me, arrays, wait_for, groups, columns)


def pass_on(me, keep_up, keep_down, far_up, far_down):
    part, columns = keep_up.shape

    def kernel(me_ref, keep_up_ref, keep_down_ref, far_up_ref, far_down_ref, up_ref, down_ref):
        def columns_step(cols):
            encode(up_ref, cols, keep_up_ref[:, cols] + decode(far_up_ref, cols, part))
            encode(down_ref, cols, keep_down_ref[:, cols] + decode(far_down_ref, cols, part))

        for_columns(columns, columns_step)

    coded = jax.ShapeDtypeStruct((coded_rows(part), columns), i16)
    return call(kernel, [coded] * 2, me, [keep_up, keep_down, far_up, far_down])


def own_sums(me, tokens, weight, near_down, sum_up, near_up, sum_down, groups, wait_for):
    share, columns = tokens.shape[0] // groups, weight.shape[1]
    part = share // 2

    def kernel(me_ref, a_ref, w_ref, near_down_ref, sum_up_ref, near_up_ref, sum_down_ref, out_ref):
        full = dot(a_ref[...], w_ref[...])
        first = decode(near_down_ref, EVERY, part) + decode(sum_up_ref, EVERY, part)
        second = decode(near_up_ref, EVERY, part) + decode(sum_down_ref, EVERY, part)
        encode(out_ref, EVERY, full + jnp.concatenate([first, second]))

    coded = jax.ShapeDtypeStruct((coded_rows(share), columns), i16)
    arrays = [(tokens, 0), weight, near_down, sum_up, near_up, sum_down]
    return by_columns(kernel, [coded], me, arrays, wait_for, groups, columns, LONG)[0]


def low_rank(me, panels, tokens, groups, ranks, distances, wait_for=()):
    sections, listed, _ = panels.shape
    rows, width = tokens.shape
    share = rows // groups
    spans = listed // ranks
    segs = spans // groups
    seg_rows = share // segs
    count = len(distances)

    def kernel(scalars_ref, panels_ref, tokens_ref, *refs):
        outs, (whole, products) = refs[:count], refs[count:]
        for i in range(sections):
            whole[:, i * LANES : (i + 1) * LANES] = panels_ref[i]
        for d in range(count):
            share_of = (scalars_ref[0] + distances[d]) % groups
            rows_here = pl.ds(pl.multiple_of(share_of * share, share), share)
            products[d] = lax.dot_general(
                whole[...],
                tokens_ref[rows_here, :],
                (((1,), (1,)), ((), ())),
                preferred_element_type=f32,
            )
            for g in range(segs):
                listed_at = scalars_ref[2 + share_of * segs + g]
                start = pl.multiple_of(listed_at * ranks, ranks)
                here = slice(g * seg_rows, (g + 1) * seg_rows)
                outs[d][:, here] = products[d, pl.ds(start, ranks), here]

    return call(
        kernel,
        [jax.ShapeDtypeStruct((ranks, share), f32)] * count,
        me,
        [panels, tokens],
        wait_for,
        scratch_shapes=[
            pltpu.VMEM((listed, width), bf16),
            pltpu.VMEM((count, listed, share), f32),
        ],
    )


def finish(me, base, arrived, expander):
    pools = len(arrived)
    ranks, share = arrived[0].shape
    segs, full_rank, columns = expander.shape
    seg_rows = share // segs
    halves = 2
    wide = columns // halves

    def kernel(me_ref, base_ref, *refs):
        low_refs, (up_ref, out_ref, low, made, sems) = refs[:pools], refs[pools:]
        for k in range(pools):
            start = pl.multiple_of((me_ref[1] + pools - k) % pools * ranks, ranks)
            low[pl.ds(start, ranks), :] = low_refs[k][...]
        values = low[...].T
        upper = values.astype(bf16)
        lower = (values - upper.astype(f32)).astype(bf16)
        copies = []
        for h in range(halves):
            cols = slice(h * wide, (h + 1) * wide)
            base_values = decode(base_ref, cols, share)
            for g in range(segs):
                here = slice(g * seg_rows, (g + 1) * seg_rows)
                panel = up_ref[g, :, cols]
                correction = dot(upper[here], panel) + dot(lower[here], panel)
                made[h, here, :] = base_values[here] + ADAPTER_SCALE * correction
            copy = pltpu.make_async_copy(made.at[h], out_ref.at[:, cols], sems.at[h])
            copy.start()
            copies.append(copy)
        for copy in copies:
            copy.wait()

    return call(
        kernel,
        jax.ShapeDtypeStruct((share, columns), f32),
        me,
        [base, *arrived, expander],
        out_specs=ANYWHERE,
        scratch_shapes=[
            pltpu.VMEM((pools * ranks, share), f32),
            pltpu.VMEM((halves, share, wide), f32),
            pltpu.SemaphoreType.DMA((halves,)),
        ],
    )


def shards(acts, output_weight, down, up, ids, positions, table):
    sections, groups, pools = (lax.axis_size(a) for a in ("section", "tensor", "pool"))
    me_t, me_p = lax.axis_index("tensor"), lax.axis_index("pool")
    me = jnp.concatenate([jnp.stack([me_t, me_p]).astype(i32), positions[0]])
    slots, ranks, _ = down.shape
    columns = up.shape[2]
    spans = ids.shape[1]
    tokens, weight = acts[0], output_weight[0]
    own_segs = spans // groups
    half = ranks // 2
    marked = slots * (ranks + half)

    spread = spread_pieces(down, up, positions)
    held = swap_all(spread, "section")
    hit = ids[:, :, None] == jnp.arange(table.shape[0], dtype=i32)
    slot_ids = jnp.sum(jnp.where(hit, table, 0), axis=-1)

    far_up, far_down = far_sums(me, tokens, weight, groups, [spread])
    near_up, near_down, keep_up, keep_down = near_sums(me, tokens, weight, groups, [far_up])
    far_up, far_down = along(far_up, "tensor", 1), along(far_down, "tensor", -1)
    near_up, near_down = along(near_up, "tensor", 1), along(near_down, "tensor", -1)
    more_up, more_down = pass_on(me, keep_up, keep_down, far_up, far_down)
    sum_up, sum_down = along(more_up, "tensor", 1), along(more_down, "tensor", -1)

    owners, starts = slot_ids // slots, slot_ids % slots * ranks
    picked_down = pick_down(held, owners, starts, ranks, [more_up])
    got_down = swap_all(picked_down, "section")
    base = own_sums(
        me, tokens, weight, near_down, sum_up, near_up, sum_down, groups, [picked_down]
    )
    all_pos = held[:, marked, :spans].astype(i32)
    seg_hit = all_pos[:, :, None] == jnp.arange(spans, dtype=i32)
    seg_slots = jnp.sum(jnp.where(seg_hit, slot_ids[:, None, :], 0), axis=-1)
    picked_up = pick_up(held, jnp.roll(seg_slots, 1, axis=0), slots, ranks, [base])
    base = to_next_section(base, 0)
    got_up = swap_all(
        picked_up.reshape(sections * groups, own_segs * half, LANES), ("section", "tensor")
    )
    expander = (
        got_up.reshape(columns // LANES, 2, groups, own_segs, half, LANES)
        .transpose(3, 2, 1, 4, 0, 5)
        .reshape(own_segs, groups * ranks, columns)
    )

    others = list(range(1, groups))
    sent = low_rank(me, got_down, tokens, groups, ranks, others)
    (reduced,) = low_rank(me, got_down, tokens, groups, ranks, [0], [sent[0]])
    for distance in others:
        reduced = reduced + along(sent[distance - 1], "tensor", distance)
    arrived = [to_next_section(reduced, k) for k in range(pools)]
    return finish(me, base, arrived, expander)[None]


def solution(mesh):
    return jax.shard_map(
        shards,
        mesh=mesh,
        in_specs=(
            P("section", None, "tensor"),
            P("section", "tensor", "pool"),
            P("section", "pool", "tensor"),
            P("section", "tensor", "pool"),
            P(),
            P("section", None),
            P(),
        ),
        out_specs=P("section", "tensor", "pool"),
        check_vma=False,
    )
```
